32 devices in a mesh: groups: 2 (over x), tensor: 8 (over z, y), replica: 2 (over core).
Axes of the slice: x: 2, y: 2, z: 4, core: 2. Of those that a mesh axis runs over, the one named last changes fastest.
Arguments:
- fresh_activations: bfloat16 [64, 4, 5120], P(('groups', 'tensor', 'replica')), parts along dimension 0, may hold values from -6 to 6
- entry_norm_multiplier: float32 [10240], P('groups'), parts along dimension 0, may hold values from 0.1 to 1.9
- base_probe_projection: bfloat16 [10240, 8192], P('groups', 'tensor'), parts along dimension 0, may hold values from -0.078125 to 0.078125
- lookup_projection: bfloat16 [10240, 1024], P('groups', 'tensor'), parts along dimension 0, may hold values from -0.078125 to 0.078125
- contents_projection: bfloat16 [10240, 1024], P('groups', 'tensor'), parts along dimension 0, may hold values from -0.078125 to 0.078125
- base_result_projection: bfloat16 [16384, 5120], P(('groups', 'tensor')), parts along dimension 0, may hold values from -0.5 to 0.5
- probe_norm_multiplier: float32 [256], P('groups'), parts along dimension 0, may hold values from 0.1 to 1.9
- lookup_norm_multiplier: float32 [256], P('groups'), parts along dimension 0, may hold values from 0.1 to 1.9
- probe_narrowing_matrix: bfloat16 [10240, 64], P(('groups', 'tensor', 'replica')), parts along dimension 0, may hold values from -0.078125 to 0.078125
- probe_widening_matrix: bfloat16 [16384, 64], P(('groups', 'tensor', 'replica')), parts along dimension 0, may hold values from -0.375 to 0.375
- result_narrowing_matrix: bfloat16 [16384, 64], P(('groups', 'tensor', 'replica')), parts along dimension 0, may hold values from -0.0625 to 0.0625
- result_widening_matrix: bfloat16 [10240, 64], P(('groups', 'tensor', 'replica')), parts along dimension 0, may hold values from -2 to 2
- stored_rotated_lookups: bfloat16 [64, 8, 384, 128], P(('groups', 'tensor', 'replica')), parts along dimension 0, may hold values from -2.5 to 2.5
- stored_contents: bfloat16 [64, 8, 384, 128], P(('groups', 'tensor', 'replica')), parts along dimension 0, may hold values from -4 to 4
- stored_extent_per_sequence: int32 [64], P(('groups', 'tensor', 'replica')), parts along dimension 0, may hold values from 1 to 384, as said below
Outputs:
- attn_output: bfloat16 [64, 4, 5120], P(('groups', 'tensor', 'replica')), parts along dimension 0
The draws below stay inside these ranges and needn't reach their ends.
There are 2 independent parts, one for each index of `groups`. The reference program is written for one: setup_inputs(seed, part) draws one part's arguments, and reference() takes and returns one part's arrays. A program takes and returns all parts, laid end to end along the dimension named above; each array names one. Nothing has to cross between parts.
Inputs may be any that keep to these rules, and one draw needn't show every extreme that they name: Row b's first stored_extent_per_sequence[b] slots are filled. In every draw the 2 rows of some aligned block of rows, which block drawn from the seed, all have length 384.
All inputs are finite; a program needn't handle non-finite values.
Results may differ from the reference program's by a relative error of at most 0.01.
Values may be sent and summed in bfloat16 or wider, within the bound.
A program may use at most 128 MiB of HBM per device.

```python
import jax
import jax.numpy as jnp
from jax import lax

HIDDEN_BREADTH = 5120
QUESTION_GROUPS = 64
KEY_VALUE_HEADS = 8
ATTN_DEPTH = 128
LOW_RANK_DIM = 64
NEW_TOKENS = 4
ROW_DEV = 2
CACHE_SLOTS = 384
DECODE_ROWS = 32


def draw_stored_extent_per_sequence(key, part):
    key = jax.random.fold_in(key, 11)
    first_key, second_key = jax.random.split(key)
    base = jax.random.randint(first_key, (DECODE_ROWS,), 1, CACHE_SLOTS + 1)
    chosen = jax.random.randint(second_key, (), 0, DECODE_ROWS // ROW_DEV)
    blocks = jnp.arange(DECODE_ROWS, dtype=jnp.int32) // ROW_DEV
    return jnp.where(blocks == chosen, CACHE_SLOTS, base).astype(jnp.int32)


def shard_levels(key, dims, pieces, smallest, top_value):
    level, own = 1.0, jax.random.fold_in(key, 6)
    for dim, shards_of in pieces:
        heights = jnp.exp(jax.random.uniform(jax.random.fold_in(own, dim), (shards_of,), jnp.float32, smallest / len(pieces), top_value / len(pieces)))
        level = level * jnp.repeat(heights, dims[dim] // shards_of).reshape([-1 if axis == dim else 1 for axis in range(len(dims))])
    return level


def centred(own_key, extent, spread, reach, pieces=(), kind=jnp.bfloat16):
    values = spread * jax.random.normal(own_key, extent, jnp.float32)
    if pieces:
        values = values * shard_levels(own_key, extent, pieces, -0.22, 0.18)
    return jnp.clip(values, -reach, reach).astype(kind)


def setup_inputs(seed: int = 0, part: int = 0) -> dict:
    seeds = jax.random.split(jax.random.key(seed), 16)
    part_keys = jax.random.split(jax.random.fold_in(seeds[15], part), 16)
    return {
        "fresh_activations": centred(part_keys[0], (DECODE_ROWS, NEW_TOKENS, HIDDEN_BREADTH), 1.0, 6.0, ((0, 16),)),
        "entry_norm_multiplier": jnp.clip(1.0 + 0.18 * jax.random.normal(part_keys[1], (HIDDEN_BREADTH,), jnp.float32), 0.1, 1.9),
        "base_probe_projection": centred(part_keys[2], (HIDDEN_BREADTH, QUESTION_GROUPS * ATTN_DEPTH), HIDDEN_BREADTH ** -0.5, 0.078125, ((1, 8),)),
        "lookup_projection": centred(part_keys[3], (HIDDEN_BREADTH, KEY_VALUE_HEADS * ATTN_DEPTH), HIDDEN_BREADTH ** -0.5, 0.078125, ((1, 8),)),
        "contents_projection": centred(part_keys[4], (HIDDEN_BREADTH, KEY_VALUE_HEADS * ATTN_DEPTH), HIDDEN_BREADTH ** -0.5, 0.078125, ((1, 8),)),
        "base_result_projection": centred(part_keys[5], (QUESTION_GROUPS * ATTN_DEPTH, HIDDEN_BREADTH), ATTN_DEPTH ** -0.5, 0.5, ((0, 8),)),
        "probe_norm_multiplier": jnp.clip(1.0 + 0.18 * jax.random.normal(part_keys[6], (ATTN_DEPTH,), jnp.float32), 0.1, 1.9),
        "lookup_norm_multiplier": jnp.clip(1.0 + 0.18 * jax.random.normal(part_keys[7], (ATTN_DEPTH,), jnp.float32), 0.1, 1.9),
        "probe_narrowing_matrix": centred(part_keys[8], (HIDDEN_BREADTH, LOW_RANK_DIM), HIDDEN_BREADTH ** -0.5, 0.078125, ((0, 16),)),
        "probe_widening_matrix": centred(part_keys[9], (QUESTION_GROUPS * ATTN_DEPTH, LOW_RANK_DIM), (4 * LOW_RANK_DIM) ** -0.5, 0.375, ((0, 16),)),
        "result_narrowing_matrix": centred(part_keys[10], (QUESTION_GROUPS * ATTN_DEPTH, LOW_RANK_DIM), (QUESTION_GROUPS * ATTN_DEPTH) ** -0.5, 0.0625, ((0, 16),)),
        "result_widening_matrix": centred(part_keys[11], (HIDDEN_BREADTH, LOW_RANK_DIM), (LOW_RANK_DIM // 8) ** -0.5, 2.0, ((0, 16),)),
        "stored_rotated_lookups": centred(part_keys[12], (DECODE_ROWS, KEY_VALUE_HEADS, CACHE_SLOTS, ATTN_DEPTH), 1.0, 2.5, ((0, 16),)),
        "stored_contents": centred(part_keys[13], (DECODE_ROWS, KEY_VALUE_HEADS, CACHE_SLOTS, ATTN_DEPTH), 1.0, 4.0, ((0, 16),)),
        "stored_extent_per_sequence": draw_stored_extent_per_sequence(jax.random.fold_in(jax.random.fold_in(seeds[15], part), 71), part),
    }


delta_multiplier = 2.0
rope_base = 1000000.0

def rms_norm(value_rows, gain):
    return value_rows * lax.rsqrt(lax.optimization_barrier(jnp.mean(value_rows * value_rows, axis=-1, keepdims=True)) + 1e-06) * gain

def rotate(value_rows, positions):
    half = value_rows.shape[-1] // 2
    freqs = rope_base ** (-(jnp.arange(half, dtype=jnp.float32) * 2.0) / value_rows.shape[-1])
    angles = positions[..., None] * freqs
    cosine = jnp.cos(angles)
    sine = jnp.sin(angles)
    first = value_rows[..., :half]
    second = value_rows[..., half:]
    return jnp.concatenate([first * cosine - second * sine, second * cosine + first * sine], axis=-1)

def attend(rot_query, rot_keys, new_values, stored_rotated_lookups, stored_contents, lengths):
    batch, token_steps, heads, width = rot_query.shape
    kv_heads = rot_keys.shape[2]
    group = heads // kv_heads
    scale = 1.0 / width ** 0.5
    query = rot_query.reshape(batch, token_steps, kv_heads, group, width).astype(jnp.float32)
    cached = jnp.einsum('bshgd,bhld->bhsgl', query, stored_rotated_lookups.astype(jnp.float32)) * scale
    fresh = jnp.einsum('bshgd,bthd->bhsgt', query, rot_keys.astype(jnp.float32)) * scale
    slots = jnp.arange(stored_rotated_lookups.shape[2], dtype=jnp.int32)
    cache_mask = (slots[None, :] < lengths[:, None])[:, None, None, None, :]
    order = jnp.arange(token_steps, dtype=jnp.int32)
    fresh_mask = (order[None, :] <= order[:, None])[None, None, :, None, :]
    cached_exp = jnp.where(cache_mask, jnp.exp(cached), 0.0)
    fresh_exp = jnp.where(fresh_mask, jnp.exp(fresh), 0.0)
    denom = lax.optimization_barrier(jnp.sum(cached_exp, axis=-1)) + lax.optimization_barrier(jnp.sum(fresh_exp, axis=-1))
    cached_w = (cached_exp / denom[..., None]).astype(jnp.bfloat16)
    fresh_w = (fresh_exp / denom[..., None]).astype(jnp.bfloat16)
    mixed = jnp.einsum('bhsgl,bhld->bshgd', cached_w.astype(jnp.float32), stored_contents.astype(jnp.float32))
    mixed = mixed + jnp.einsum('bhsgt,bthd->bshgd', fresh_w.astype(jnp.float32), new_values.astype(jnp.float32))
    return mixed.reshape(batch, token_steps, heads * width).astype(jnp.bfloat16)

def reference(fresh_activations, entry_norm_multiplier, base_probe_projection, lookup_projection, contents_projection, base_result_projection, probe_norm_multiplier, lookup_norm_multiplier, probe_narrowing_matrix, probe_widening_matrix, result_narrowing_matrix, result_widening_matrix, stored_rotated_lookups, stored_contents, stored_extent_per_sequence):
    normed = rms_norm(fresh_activations.astype(jnp.float32), entry_norm_multiplier).astype(jnp.bfloat16)
    merged_probe_projection = (base_probe_projection.astype(jnp.float32) + delta_multiplier * jnp.dot(probe_narrowing_matrix, probe_widening_matrix.T, preferred_element_type=jnp.float32)).astype(jnp.bfloat16)
    merged_projection_back = (base_result_projection.astype(jnp.float32) + delta_multiplier * jnp.dot(result_narrowing_matrix, result_widening_matrix.T, preferred_element_type=jnp.float32)).astype(jnp.bfloat16)
    flattened_rows = normed.reshape(DECODE_ROWS * NEW_TOKENS, HIDDEN_BREADTH)
    query = jnp.dot(flattened_rows, merged_probe_projection, preferred_element_type=jnp.float32).astype(jnp.bfloat16).reshape(DECODE_ROWS, NEW_TOKENS, QUESTION_GROUPS, ATTN_DEPTH)
    key_rows = jnp.dot(flattened_rows, lookup_projection, preferred_element_type=jnp.float32).astype(jnp.bfloat16).reshape(DECODE_ROWS, NEW_TOKENS, KEY_VALUE_HEADS, ATTN_DEPTH)
    value_rows = jnp.dot(flattened_rows, contents_projection, preferred_element_type=jnp.float32).astype(jnp.bfloat16).reshape(DECODE_ROWS, NEW_TOKENS, KEY_VALUE_HEADS, ATTN_DEPTH)
    positions = (stored_extent_per_sequence[:, None] + jnp.arange(NEW_TOKENS, dtype=jnp.int32)[None, :]).astype(jnp.float32)[:, :, None]
    rot_query = rotate(rms_norm(query.astype(jnp.float32), probe_norm_multiplier), positions).astype(jnp.bfloat16)
    rot_keys = rotate(rms_norm(key_rows.astype(jnp.float32), lookup_norm_multiplier), positions).astype(jnp.bfloat16)
    attended = attend(rot_query, rot_keys, value_rows, stored_rotated_lookups, stored_contents, stored_extent_per_sequence)
    result = jnp.dot(attended.reshape(DECODE_ROWS * NEW_TOKENS, QUESTION_GROUPS * ATTN_DEPTH), merged_projection_back, preferred_element_type=jnp.float32)
    return result.astype(jnp.bfloat16).reshape(DECODE_ROWS, NEW_TOKENS, HIDDEN_BREADTH)
```

```python
import functools
import math

import jax
import jax.numpy as jnp
from jax import lax
from jax.experimental import pallas as pl
from jax.experimental.pallas import tpu as pltpu
from jax.sharding import PartitionSpec as P

QUESTION_GROUPS = 64
KEY_VALUE_HEADS = 8
ATTN_DEPTH = 128


delta_multiplier = 2.0
rope_base = 1000000.0


def rms_norm(value_rows, gain):
    return (
        value_rows
        * lax.rsqrt(jnp.mean(value_rows * value_rows, axis=-1, keepdims=True) + 1e-06)
        * gain
    )


def rotate(value_rows, positions):
    half = value_rows.shape[-1] // 2
    freqs = rope_base ** (-(jnp.arange(half, dtype=jnp.float32) * 2.0) / value_rows.shape[-1])
    angles = positions[..., None] * freqs
    cosine = jnp.cos(angles)
    sine = jnp.sin(angles)
    first = value_rows[..., :half]
    second = value_rows[..., half:]
    return jnp.concatenate(
        [first * cosine - second * sine, second * cosine + first * sine], axis=-1
    )


def attend(rot_query, rot_keys, new_values, stored_rotated_lookups, stored_contents, lengths):
    batch, token_steps, heads, width = rot_query.shape
    kv_heads = rot_keys.shape[2]
    group = heads // kv_heads
    scale = 1.0 / width**0.5
    query = rot_query.reshape(batch, token_steps, kv_heads, group, width)
    cached = (
        jnp.einsum(
            "bshgd,bhld->bhsgl", query, stored_rotated_lookups, preferred_element_type=jnp.float32
        )
        * scale
    )
    fresh = (
        jnp.einsum("bshgd,bthd->bhsgt", query, rot_keys, preferred_element_type=jnp.float32) * scale
    )
    slots = jnp.arange(stored_rotated_lookups.shape[2], dtype=jnp.int32)
    cache_mask = (slots[None, :] < lengths[:, None])[:, None, None, None, :]
    order = jnp.arange(token_steps, dtype=jnp.int32)
    fresh_mask = (order[None, :] <= order[:, None])[None, None, :, None, :]
    cached_exp = jnp.where(cache_mask, jnp.exp(cached), 0.0)
    fresh_exp = jnp.where(fresh_mask, jnp.exp(fresh), 0.0)
    denom = jnp.sum(cached_exp, axis=-1) + jnp.sum(fresh_exp, axis=-1)
    cached_w = (cached_exp / denom[..., None]).astype(jnp.bfloat16)
    fresh_w = (fresh_exp / denom[..., None]).astype(jnp.bfloat16)
    mixed = jnp.einsum(
        "bhsgl,bhld->bshgd", cached_w, stored_contents, preferred_element_type=jnp.float32
    )
    mixed = mixed + jnp.einsum(
        "bhsgt,bthd->bshgd", fresh_w, new_values, preferred_element_type=jnp.float32
    )
    return mixed.reshape(batch, token_steps, heads * width).astype(jnp.bfloat16)


def gather_pieces(wide, narrow):
    distribute_pieces = (
        lax.all_gather(wide[0], ("tensor", "replica"), axis=0, tiled=True),
        lax.all_gather(wide[1], ("tensor", "replica"), axis=0, tiled=True),
    )
    device_portion = (
        lax.all_gather(narrow[0], "replica", axis=0, tiled=True),
        lax.all_gather(narrow[1], "replica", axis=0, tiled=True),
    )
    return (distribute_pieces, device_portion)


def body(
    fresh_activations,
    entry_norm_multiplier,
    base_probe_projection,
    lookup_projection,
    contents_projection,
    base_result_projection,
    probe_norm_multiplier,
    lookup_norm_multiplier,
    probe_narrowing_matrix,
    probe_widening_matrix,
    result_narrowing_matrix,
    result_widening_matrix,
    stored_rotated_lookups,
    stored_contents,
    stored_extent_per_sequence,
):
    decode_row_count, token_steps, width = fresh_activations.shape
    normed = rms_norm(fresh_activations.astype(jnp.float32), entry_norm_multiplier).astype(
        jnp.bfloat16
    )
    distribute_pieces, device_portion = gather_pieces(
        (probe_narrowing_matrix, result_widening_matrix),
        (probe_widening_matrix, result_narrowing_matrix),
    )
    query_down_factor, output_up_factor = distribute_pieces
    query_up_factor, output_down_factor = device_portion
    merged_projection_back = (
        base_result_projection.astype(jnp.float32)
        + delta_multiplier
        * jnp.dot(output_down_factor, output_up_factor.T, preferred_element_type=jnp.float32)
    ).astype(jnp.bfloat16)
    merged_probe_projection = (
        base_probe_projection.astype(jnp.float32)
        + delta_multiplier
        * jnp.dot(query_down_factor, query_up_factor.T, preferred_element_type=jnp.float32)
    ).astype(jnp.bfloat16)
    packed = jnp.concatenate(
        [merged_probe_projection, lookup_projection, contents_projection], axis=1
    )
    query_feature_width = merged_probe_projection.shape[1]
    key_feature_width = lookup_projection.shape[1]
    packed_width = packed.shape[1]
    piece = lax.all_gather(normed, "tensor", axis=0, tiled=True)
    piece_rows = piece.shape[0]
    flattened_rows = piece.reshape(piece_rows * token_steps, width)
    projected = (
        jnp.dot(flattened_rows, packed, preferred_element_type=jnp.float32)
        .astype(jnp.bfloat16)
        .reshape(piece_rows, token_steps, packed_width)
    )
    received_shards = lax.all_to_all(projected, "tensor", split_axis=0, concat_axis=2, tiled=True)
    shards = lax.axis_size("tensor")
    received_shards = received_shards.reshape(decode_row_count, token_steps, shards, packed_width)
    query = received_shards[..., :query_feature_width].reshape(
        decode_row_count, token_steps, QUESTION_GROUPS, ATTN_DEPTH
    )
    key_rows = received_shards[
        ..., query_feature_width : query_feature_width + key_feature_width
    ].reshape(decode_row_count, token_steps, KEY_VALUE_HEADS, ATTN_DEPTH)
    value_rows = received_shards[..., query_feature_width + key_feature_width :].reshape(
        decode_row_count, token_steps, KEY_VALUE_HEADS, ATTN_DEPTH
    )
    positions = (
        stored_extent_per_sequence[:, None] + jnp.arange(token_steps, dtype=jnp.int32)[None, :]
    ).astype(jnp.float32)[:, :, None]
    rot_query = rotate(
        rms_norm(query.astype(jnp.float32), probe_norm_multiplier), positions
    ).astype(jnp.bfloat16)
    rot_keys = rotate(
        rms_norm(key_rows.astype(jnp.float32), lookup_norm_multiplier), positions
    ).astype(jnp.bfloat16)
    attended = attend(
        rot_query,
        rot_keys,
        value_rows,
        stored_rotated_lookups,
        stored_contents,
        stored_extent_per_sequence,
    )
    returned = lax.all_to_all(attended, "tensor", split_axis=2, concat_axis=0, tiled=True)
    amount = decode_row_count * lax.axis_size("tensor")
    flattened_rows = returned.reshape(amount * token_steps, returned.shape[2])
    total = lax.psum_scatter(
        jnp.dot(flattened_rows, merged_projection_back, preferred_element_type=jnp.float32).reshape(
            amount, token_steps, width
        ),
        "tensor",
        scatter_dimension=0,
        tiled=True,
    )
    return total.astype(jnp.bfloat16)


BF16 = jnp.bfloat16
F32 = jnp.float32
MESH = pl.DeviceIdType.MESH


def dot_nn(a, b):
    return jnp.dot(a, b, preferred_element_type=F32)


def dot_nt(a, b):
    return lax.dot_general(a, b, (((1,), (1,)), ((), ())), preferred_element_type=F32)


def fused_kernel(
    n,
    x_ref, gain_ref, wq_ref, wk_ref, wv_ref, wo_ref, qgain_ref, kgain_ref,
    a_ref, b_ref, c_ref, d_ref, kc_ref, vc_ref, len_ref,
    out_ref,
    xs, w, wo, kbuf, vbuf, a2, b1, c2, d2, ts, us, acc, qs, qr, att_src, ar, abf, ps, rr, half_out, half_in,
    loc, x_s, x_f, x_r, t_s, t_r, q_s, q_r, a_s, a_f, a_r, u_s, u_r, p_s, p_r, m_s, m_r,
):
    i = lax.axis_index("tensor")
    r = lax.axis_index("replica")
    o = 1 - r
    me = 2 * i + r
    width = x_ref.shape[1]
    qcols = w.shape[1] - ATTN_DEPTH
    ocols = wo.shape[1]
    chunk = rr.shape[3]
    chunks = ocols // chunk
    slots_len = kc_ref.shape[2]

    def peer(j, core):
        return {"tensor": j, "replica": core}

    def remote(src, dst, ssem, rsem, j, core):
        return pltpu.make_async_remote_copy(
            src_ref=src, dst_ref=dst, send_sem=ssem, recv_sem=rsem,
            device_id=peer(j, core), device_id_type=MESH,
        )

    def ahead(d):
        return lax.rem(i + d, n)

    def behind(d):
        return lax.rem(i + n - d, n)

    barrier = pltpu.get_barrier_semaphore()

    @pl.loop(1, 2 * n)
    def _(d):
        dev = lax.rem(me + d, 2 * n)
        pl.semaphore_signal(barrier, inc=1, device_id=peer(dev // 2, lax.rem(dev, 2)), device_id_type=MESH)

    cp_w = pltpu.make_async_copy(wq_ref.at[:, pl.ds(pl.multiple_of(r * qcols, 128), qcols)], w.at[:, pl.ds(0, qcols)], loc.at[0])
    cp_w.start()
    wkv_dst = w.at[:, pl.ds(qcols, ATTN_DEPTH)]
    cp_k = pltpu.make_async_copy(wk_ref, wkv_dst, loc.at[1])
    cp_v = pltpu.make_async_copy(wv_ref, wkv_dst, loc.at[1])

    @pl.when(r == 0)
    def _():
        cp_k.start()

    @pl.when(r == 1)
    def _():
        cp_v.start()

    small = [
        pltpu.make_async_copy(a_ref, a2.at[r], loc.at[2]),
        pltpu.make_async_copy(b_ref, b1, loc.at[3]),
        pltpu.make_async_copy(c_ref, c2.at[r], loc.at[4]),
        pltpu.make_async_copy(d_ref, d2.at[r], loc.at[5]),
    ]
    caches = []
    for b in range(2):
        caches.append(pltpu.make_async_copy(kc_ref.at[b], kbuf.at[:, pl.ds(b * slots_len, slots_len), :], loc.at[6 + b]))
        caches.append(pltpu.make_async_copy(vc_ref.at[b], vbuf.at[:, pl.ds(b * slots_len, slots_len), :], loc.at[8 + b]))
    cp_wo = pltpu.make_async_copy(wo_ref.at[:, pl.ds(pl.multiple_of(r * ocols, 128), ocols)], wo, loc.at[10])
    for cp in small + caches + [cp_wo]:
        cp.start()

    xf = x_ref[...].astype(F32)
    inv = lax.rsqrt(jnp.mean(xf * xf, axis=-1, keepdims=True) + 1e-06)
    xs[me] = (xf * inv * gain_ref[...]).astype(BF16)

    pl.semaphore_wait(barrier, 2 * n - 1)

    def x_direct(d):
        return remote(xs.at[me], xs.at[me], x_s.at[d], x_r.at[me], ahead(d), r)

    x_pair = remote(xs.at[me], xs.at[me], x_s.at[0], x_r.at[me], i, o)

    @pl.loop(1, n)
    def _(d):
        x_direct(d).start()

    x_pair.start()
    lora_pair = [
        remote(a_ref, a2.at[r], m_s.at[0], m_r.at[0], i, o),
        remote(c_ref, c2.at[r], m_s.at[1], m_r.at[1], i, o),
        remote(d_ref, d2.at[r], m_s.at[2], m_r.at[2], i, o),
    ]
    for cp in lora_pair:
        cp.start()

    row8 = lax.broadcasted_iota(jnp.int32, (8, ATTN_DEPTH), 0)
    lane8 = lax.broadcasted_iota(jnp.int32, (8, ATTN_DEPTH), 1)
    len0, len1 = len_ref[0], len_ref[1]
    pos = (jnp.where(row8 < 4, len0, len1) + lax.rem(row8, 4)).astype(F32)
    half_i = lax.rem(lane8, ATTN_DEPTH // 2).astype(F32)
    freq = jnp.exp(half_i * (-2.0 / ATTN_DEPTH * math.log(rope_base)))
    ang = pos * freq
    cos8 = jnp.cos(ang)
    sin8 = jnp.where(lane8 < ATTN_DEPTH // 2, -jnp.sin(ang), jnp.sin(ang))
    kbuf[:, pl.ds(2 * slots_len, 128), :] = jnp.zeros((n, 128, ATTN_DEPTH), BF16)
    vbuf[:, pl.ds(2 * slots_len, 128), :] = jnp.zeros((n, 128, ATTN_DEPTH), BF16)

    def x_fwd(d, j):
        s = 2 * j + r
        return remote(xs.at[s], xs.at[s], x_f.at[d], x_r.at[s], i, o)

    def x_arr(s):
        return remote(xs.at[s], xs.at[s], x_s.at[0], x_r.at[s], i, o)

    @pl.loop(1, n)
    def _(d):
        j = behind(d)
        x_arr(2 * j + r).wait_recv()
        x_fwd(d, j).start()

    @pl.loop(0, n)
    def _(d):
        x_arr(2 * behind(d) + o).wait_recv()

    def x_rows(k):
        v = xs[:, :, pl.ds(pl.multiple_of(k * 640, 128), 640)]
        return v.astype(F32).reshape(16 * 8, 640).astype(BF16)

    def pack(t):
        h = t.shape[0] // 2
        return jnp.concatenate([t[:h], t[h:]], axis=1)

    def unpack(t):
        h = t.shape[1] // 2
        return jnp.concatenate([t[:, :h], t[:, h:]], axis=0)

    small[0].wait()
    lora_pair[0].wait_recv()
    t_mine = dot_nn(x_rows(i), a2[...].reshape(640, a2.shape[2]))
    ts[i] = pack(t_mine).astype(BF16)

    def t_copy(d):
        return remote(ts.at[i], ts.at[i], t_s.at[d], t_r.at[i], ahead(d), r)

    def t_arr(s):
        return remote(ts.at[s], ts.at[s], t_s.at[0], t_r.at[s], i, o)

    @pl.loop(1, n)
    def _(d):
        t_copy(d).start()

    cp_w.wait()
    cp_k.wait()
    acc[...] = jnp.zeros_like(acc)

    @pl.loop(0, width // 640)
    def _(k):
        acc[...] += dot_nn(x_rows(k), w[pl.ds(pl.multiple_of(k * 640, 128), 640), :])

    @pl.loop(1, n)
    def _(d):
        t_arr(behind(d)).wait_recv()

    small[1].wait()
    t_all = unpack(jnp.sum(ts[...].astype(F32), axis=0)).astype(BF16)
    acc[:, pl.ds(0, qcols)] += delta_multiplier * dot_nt(t_all, b1[...])
    proj = acc[...].reshape(16, 8, w.shape[1]).astype(BF16)
    qs[...] = proj

    def q_copy(d):
        dev = lax.rem(me + d, 2 * n)
        return remote(qs.at[dev], qr.at[me], q_s.at[d], q_r.at[me], dev // 2, lax.rem(dev, 2))

    def q_arr(s):
        return remote(qr.at[s], qr.at[s], q_s.at[0], q_r.at[s], i, o)

    @pl.loop(1, 2 * n)
    def _(d):
        q_copy(d).start()

    qr[me] = qs[me]

    @pl.loop(1, 2 * n)
    def _(d):
        q_arr(lax.rem(me + 2 * n - d, 2 * n)).wait_recv()

    for cp in caches:
        cp.wait()

    heads = qcols // ATTN_DEPTH
    rows = 2 * heads * 8
    cos_q = jnp.concatenate([cos8] * (2 * heads), axis=0)
    sin_q = jnp.concatenate([sin8] * (2 * heads), axis=0)
    rb = lax.rem(lax.broadcasted_iota(jnp.int32, (rows, slots_len), 0), 8) // 4
    cache_ok = lax.broadcasted_iota(jnp.int32, (rows, slots_len), 1) < jnp.where(rb == 0, len0, len1)
    first_row = rb == 0
    fr = lax.rem(lax.broadcasted_iota(jnp.int32, (rows, 128), 0), 8)
    fc = lax.broadcasted_iota(jnp.int32, (rows, 128), 1)
    fresh_ok = (fc // 4 == fr // 4) & (lax.rem(fc, 4) <= lax.rem(fr, 4))
    scale = 1.0 / ATTN_DEPTH**0.5

    def norm_rotate(v, gain, cosine, sine):
        v = v * lax.rsqrt(jnp.mean(v * v, axis=-1, keepdims=True) + 1e-06) * gain
        return (v * cosine + pltpu.roll(v, ATTN_DEPTH // 2, 1) * sine).astype(BF16)

    def a_direct(j, d):
        return remote(att_src.at[j], ar.at[me], a_s.at[d], a_r.at[me], j, r)

    a_pair = remote(ar.at[me], ar.at[me], a_s.at[0], a_r.at[me], i, o)

    def head_group(j):
        q0 = qr[2 * j].astype(F32)
        q1 = qr[2 * j + 1].astype(F32)
        qh = jnp.concatenate(
            [q[:, h * ATTN_DEPTH : (h + 1) * ATTN_DEPTH] for q in (q0, q1) for h in range(heads)], axis=0
        )
        q = norm_rotate(qh, qgain_ref[...], cos_q, sin_q)
        kn = norm_rotate(q0[:, qcols:], kgain_ref[...], cos8, sin8).astype(F32)
        pad = jnp.zeros((8, ATTN_DEPTH), F32)
        kbuf[j, pl.ds(2 * slots_len, 16), :] = jnp.concatenate([kn, pad], axis=0).astype(BF16)
        vbuf[j, pl.ds(2 * slots_len, 16), :] = jnp.concatenate([q1[:, qcols:], pad], axis=0).astype(BF16)
        s = dot_nt(q, kbuf[j]) * scale
        cached = jnp.where(first_row, s[:, :slots_len], s[:, slots_len : 2 * slots_len])
        ec = jnp.where(cache_ok, jnp.exp(cached), 0.0)
        ef = jnp.where(fresh_ok, jnp.exp(s[:, 2 * slots_len :]), 0.0)
        denom = jnp.sum(ec, axis=-1, keepdims=True) + jnp.sum(ef, axis=-1, keepdims=True)
        wc = ec / denom
        wf = ef / denom
        wgt = jnp.concatenate(
            [jnp.where(first_row, wc, 0.0), jnp.where(first_row, 0.0, wc), wf], axis=1
        ).astype(BF16)
        o_ = dot_nn(wgt, vbuf[j])
        return jnp.concatenate([o_[h * 8 : (h + 1) * 8] for h in range(2 * heads)], axis=1).astype(BF16)

    @pl.loop(1, n)
    def _(d):
        j = ahead(d)
        att_src[j] = head_group(j)
        a_direct(j, d).start()

    ar[me] = head_group(i)
    a_pair.start()

    def a_arr(s):
        return remote(ar.at[s], ar.at[s], a_s.at[0], a_r.at[s], i, o)

    def a_fwd(d, j):
        s = 2 * j + r
        return remote(ar.at[s], ar.at[s], a_f.at[d], a_r.at[s], i, o)

    @pl.loop(1, n)
    def _(d):
        j = behind(d)
        a_arr(2 * j + r).wait_recv()
        a_fwd(d, j).start()

    @pl.loop(0, n)
    def _(d):
        a_arr(2 * behind(d) + o).wait_recv()

    abf[...] = ar[...].astype(F32).reshape(16 * 8, ar.shape[2]).astype(BF16)
    small[2].wait()
    lora_pair[1].wait_recv()
    us[i] = pack(dot_nn(abf[...], c2[...].reshape(ar.shape[2], c2.shape[2]))).astype(BF16)

    def u_copy(d):
        return remote(us.at[i], us.at[i], u_s.at[d], u_r.at[i], ahead(d), r)

    def u_arr(s):
        return remote(us.at[s], us.at[s], u_s.at[0], u_r.at[s], i, o)

    @pl.loop(1, n)
    def _(d):
        u_copy(d).start()

    cp_wo.wait()
    small[3].wait()
    lora_pair[2].wait_recv()
    own_chunk = lax.rem(i, chunks)

    def p_copy(cc, d):
        j = ahead(d)
        return remote(ps.at[cc, j], rr.at[cc, i], p_s.at[cc, d], p_r.at[cc, i], j, r)

    def p_arr(cc, s):
        return remote(rr.at[cc, s], rr.at[cc, s], p_s.at[0, 0], p_r.at[cc, s], i, o)

    def base(cc):
        return dot_nn(abf[...], wo[:, pl.ds(pl.multiple_of(cc * chunk, 128), chunk)])

    def ship(cc, part):
        ps[cc] = part.astype(BF16).reshape(n, 16, chunk)

        @pl.loop(1, n)
        def _(d):
            p_copy(cc, d).start()

    @pl.loop(1, chunks)
    def _(c):
        cc = lax.rem(own_chunk + c, chunks)
        ship(cc, base(cc))

    last = base(own_chunk)

    @pl.loop(1, n)
    def _(d):
        u_arr(behind(d)).wait_recv()

    u_all = unpack(jnp.sum(us[...].astype(F32), axis=0)).astype(BF16)
    mult = jnp.where(i // chunks == r, delta_multiplier, 0.0)
    ship(own_chunk, last + mult * dot_nt(u_all, d2[...].reshape(640, d2.shape[2])))

    @pl.loop(0, chunks)
    def _(cc):
        @pl.loop(1, n)
        def _(d):
            p_arr(cc, behind(d)).wait_recv()

        rr[cc, i] = ps[cc, i]
        total = jnp.sum(rr[cc].astype(F32), axis=0).reshape(2, 8, chunk)
        mine = jnp.where(r == 0, total[0], total[1])
        theirs = jnp.where(r == 0, total[1], total[0])
        half_out[cc] = theirs
        out_ref[:, pl.ds(pl.multiple_of(r * ocols + cc * chunk, 128), chunk)] = mine.astype(BF16)
        remote(half_out.at[cc], half_in.at[cc], m_s.at[3 + cc], m_r.at[3 + cc], i, o).start()

    @pl.loop(0, chunks)
    def _(cc):
        remote(half_out.at[cc], half_in.at[cc], m_s.at[3 + cc], m_r.at[3 + cc], i, o).wait()
        out_ref[:, pl.ds(pl.multiple_of(o * ocols + cc * chunk, 128), chunk)] = half_in[cc].astype(BF16)

    for cp in lora_pair:
        cp.wait_send()
    x_pair.wait_send()
    a_pair.wait_send()

    @pl.loop(1, n)
    def _(d):
        x_direct(d).wait_send()
        x_fwd(d, behind(d)).wait_send()
        t_copy(d).wait_send()
        a_direct(ahead(d), d).wait_send()
        a_fwd(d, behind(d)).wait_send()
        u_copy(d).wait_send()
        for cc in range(chunks):
            p_copy(cc, d).wait_send()

    @pl.loop(1, 2 * n)
    def _(d):
        q_copy(d).wait_send()


def fused_body(
    n,
    fresh_activations,
    entry_norm_multiplier,
    base_probe_projection,
    lookup_projection,
    contents_projection,
    base_result_projection,
    probe_norm_multiplier,
    lookup_norm_multiplier,
    probe_narrowing_matrix,
    probe_widening_matrix,
    result_narrowing_matrix,
    result_widening_matrix,
    stored_rotated_lookups,
    stored_contents,
    stored_extent_per_sequence,
):
    rows_dev, steps, width = fresh_activations.shape
    rows = rows_dev * steps
    qcols = base_probe_projection.shape[1] // 2
    ocols = width // 2
    feats = base_result_projection.shape[0]
    rank = probe_narrowing_matrix.shape[1]
    part, up = probe_narrowing_matrix.shape[0], probe_widening_matrix.shape[0]
    slots = stored_rotated_lookups.shape[2]
    chunk = 2 * part
    chunks = ocols // chunk
    vmem = pl.BlockSpec(memory_space=pltpu.VMEM)
    hbm = pl.BlockSpec(memory_space=pl.ANY)
    smem = pl.BlockSpec(memory_space=pltpu.SMEM)
    dma = pltpu.SemaphoreType.DMA
    out = pl.pallas_call(
        functools.partial(fused_kernel, n),
        out_shape=jax.ShapeDtypeStruct((rows, width), BF16),
        in_specs=[vmem, vmem, hbm, hbm, hbm, hbm, vmem, vmem, hbm, hbm, hbm, hbm, hbm, hbm, smem],
        out_specs=vmem,
        scratch_shapes=[
            pltpu.VMEM((2 * n, rows, width), BF16),
            pltpu.VMEM((width, qcols + ATTN_DEPTH), BF16),
            pltpu.VMEM((feats, ocols), BF16),
            pltpu.VMEM((n, 2 * slots + 128, ATTN_DEPTH), BF16),
            pltpu.VMEM((n, 2 * slots + 128, ATTN_DEPTH), BF16),
            pltpu.VMEM((2, part, rank), BF16),
            pltpu.VMEM((up, rank), BF16),
            pltpu.VMEM((2, up, rank), BF16),
            pltpu.VMEM((2, part, rank), BF16),
            pltpu.VMEM((n, n * rows, 2 * rank), BF16),
            pltpu.VMEM((n, n * rows, 2 * rank), BF16),
            pltpu.VMEM((2 * n * rows, qcols + ATTN_DEPTH), F32),
            pltpu.VMEM((2 * n, rows, qcols + ATTN_DEPTH), BF16),
            pltpu.VMEM((2 * n, rows, qcols + ATTN_DEPTH), BF16),
            pltpu.VMEM((n, rows, feats), BF16),
            pltpu.VMEM((2 * n, rows, feats), BF16),
            pltpu.VMEM((2 * n * rows, feats), BF16),
            pltpu.VMEM((chunks, n, 2 * rows, chunk), BF16),
            pltpu.VMEM((chunks, n, 2 * rows, chunk), BF16),
            pltpu.VMEM((chunks, rows, chunk), F32),
            pltpu.VMEM((chunks, rows, chunk), F32),
            dma((11,)),
            dma((n,)), dma((n,)), dma((2 * n,)),
            dma((n,)), dma((n,)),
            dma((2 * n,)), dma((2 * n,)),
            dma((n,)), dma((n,)), dma((2 * n,)),
            dma((n,)), dma((n,)),
            dma((chunks, n)), dma((chunks, n)),
            dma((3 + chunks,)), dma((3 + chunks,)),
        ],
        compiler_params=pltpu.CompilerParams(
            collective_id=0, has_side_effects=True, vmem_limit_bytes=56 * 1024 * 1024
        ),
        name="fused_attention_sync",
    )(
        fresh_activations.reshape(rows, width),
        entry_norm_multiplier.reshape(1, width),
        base_probe_projection,
        lookup_projection,
        contents_projection,
        base_result_projection,
        probe_norm_multiplier.reshape(1, ATTN_DEPTH),
        lookup_norm_multiplier.reshape(1, ATTN_DEPTH),
        probe_narrowing_matrix,
        probe_widening_matrix,
        result_narrowing_matrix,
        result_widening_matrix,
        stored_rotated_lookups,
        stored_contents,
        stored_extent_per_sequence,
    )
    return out.reshape(rows_dev, steps, width)


def solution(mesh):
    n = mesh.shape["tensor"]
    fits = n == KEY_VALUE_HEADS and mesh.shape["replica"] == 2
    return jax.shard_map(
        functools.partial(fused_body, n) if fits else body,
        mesh=mesh,
        in_specs=(
            P(("groups", "tensor", "replica"), None, None),
            P("groups"),
            P("groups", "tensor"),
            P("groups", "tensor"),
            P("groups", "tensor"),
            P(("groups", "tensor"), None),
            P("groups"),
            P("groups"),
            P(("groups", "tensor", "replica"), None),
            P(("groups", "tensor", "replica"), None),
            P(("groups", "tensor", "replica"), None),
            P(("groups", "tensor", "replica"), None),
            P(("groups", "tensor", "replica"), None, None, None),
            P(("groups", "tensor", "replica"), None, None, None),
            P(("groups", "tensor", "replica")),
        ),
        out_specs=P(("groups", "tensor", "replica"), None, None),
        check_vma=False,
    )
```

```python
import functools
import math

import jax
import jax.numpy as jnp
from jax import lax
from jax.experimental import pallas as pl
from jax.experimental.pallas import tpu as pltpu
from jax.sharding import PartitionSpec as P

QUESTION_GROUPS = 64
KEY_VALUE_HEADS = 8
ATTN_DEPTH = 128


delta_multiplier = 2.0
rope_base = 1000000.0


def rms_norm(value_rows, gain):
    return (
        value_rows
        * lax.rsqrt(jnp.mean(value_rows * value_rows, axis=-1, keepdims=True) + 1e-06)
        * gain
    )


def rotate(value_rows, positions):
    half = value_rows.shape[-1] // 2
    freqs = rope_base ** (-(jnp.arange(half, dtype=jnp.float32) * 2.0) / value_rows.shape[-1])
    angles = positions[..., None] * freqs
    cosine = jnp.cos(angles)
    sine = jnp.sin(angles)
    first = value_rows[..., :half]
    second = value_rows[..., half:]
    return jnp.concatenate(
        [first * cosine - second * sine, second * cosine + first * sine], axis=-1
    )


def attend(rot_query, rot_keys, new_values, stored_rotated_lookups, stored_contents, lengths):
    batch, token_steps, heads, width = rot_query.shape
    kv_heads = rot_keys.shape[2]
    group = heads // kv_heads
    scale = 1.0 / width**0.5
    query = rot_query.reshape(batch, token_steps, kv_heads, group, width)
    cached = (
        jnp.einsum(
            "bshgd,bhld->bhsgl", query, stored_rotated_lookups, preferred_element_type=jnp.float32
        )
        * scale
    )
    fresh = (
        jnp.einsum("bshgd,bthd->bhsgt", query, rot_keys, preferred_element_type=jnp.float32) * scale
    )
    slots = jnp.arange(stored_rotated_lookups.shape[2], dtype=jnp.int32)
    cache_mask = (slots[None, :] < lengths[:, None])[:, None, None, None, :]
    order = jnp.arange(token_steps, dtype=jnp.int32)
    fresh_mask = (order[None, :] <= order[:, None])[None, None, :, None, :]
    cached_exp = jnp.where(cache_mask, jnp.exp(cached), 0.0)
    fresh_exp = jnp.where(fresh_mask, jnp.exp(fresh), 0.0)
    denom = jnp.sum(cached_exp, axis=-1) + jnp.sum(fresh_exp, axis=-1)
    cached_w = (cached_exp / denom[..., None]).astype(jnp.bfloat16)
    fresh_w = (fresh_exp / denom[..., None]).astype(jnp.bfloat16)
    mixed = jnp.einsum(
        "bhsgl,bhld->bshgd", cached_w, stored_contents, preferred_element_type=jnp.float32
    )
    mixed = mixed + jnp.einsum(
        "bhsgt,bthd->bshgd", fresh_w, new_values, preferred_element_type=jnp.float32
    )
    return mixed.reshape(batch, token_steps, heads * width).astype(jnp.bfloat16)


def gather_pieces(wide, narrow):
    distribute_pieces = (
        lax.all_gather(wide[0], ("tensor", "replica"), axis=0, tiled=True),
        lax.all_gather(wide[1], ("tensor", "replica"), axis=0, tiled=True),
    )
    device_portion = (
        lax.all_gather(narrow[0], "replica", axis=0, tiled=True),
        lax.all_gather(narrow[1], "replica", axis=0, tiled=True),
    )
    return (distribute_pieces, device_portion)


def body(
    fresh_activations,
    entry_norm_multiplier,
    base_probe_projection,
    lookup_projection,
    contents_projection,
    base_result_projection,
    probe_norm_multiplier,
    lookup_norm_multiplier,
    probe_narrowing_matrix,
    probe_widening_matrix,
    result_narrowing_matrix,
    result_widening_matrix,
    stored_rotated_lookups,
    stored_contents,
    stored_extent_per_sequence,
):
    decode_row_count, token_steps, width = fresh_activations.shape
    normed = rms_norm(fresh_activations.astype(jnp.float32), entry_norm_multiplier).astype(
        jnp.bfloat16
    )
    distribute_pieces, device_portion = gather_pieces(
        (probe_narrowing_matrix, result_widening_matrix),
        (probe_widening_matrix, result_narrowing_matrix),
    )
    query_down_factor, output_up_factor = distribute_pieces
    query_up_factor, output_down_factor = device_portion
    merged_projection_back = (
        base_result_projection.astype(jnp.float32)
        + delta_multiplier
        * jnp.dot(output_down_factor, output_up_factor.T, preferred_element_type=jnp.float32)
    ).astype(jnp.bfloat16)
    merged_probe_projection = (
        base_probe_projection.astype(jnp.float32)
        + delta_multiplier
        * jnp.dot(query_down_factor, query_up_factor.T, preferred_element_type=jnp.float32)
    ).astype(jnp.bfloat16)
    packed = jnp.concatenate(
        [merged_probe_projection, lookup_projection, contents_projection], axis=1
    )
    query_feature_width = merged_probe_projection.shape[1]
    key_feature_width = lookup_projection.shape[1]
    packed_width = packed.shape[1]
    piece = lax.all_gather(normed, "tensor", axis=0, tiled=True)
    piece_rows = piece.shape[0]
    flattened_rows = piece.reshape(piece_rows * token_steps, width)
    projected = (
        jnp.dot(flattened_rows, packed, preferred_element_type=jnp.float32)
        .astype(jnp.bfloat16)
        .reshape(piece_rows, token_steps, packed_width)
    )
    received_shards = lax.all_to_all(projected, "tensor", split_axis=0, concat_axis=2, tiled=True)
    shards = lax.axis_size("tensor")
    received_shards = received_shards.reshape(decode_row_count, token_steps, shards, packed_width)
    query = received_shards[..., :query_feature_width].reshape(
        decode_row_count, token_steps, QUESTION_GROUPS, ATTN_DEPTH
    )
    key_rows = received_shards[
        ..., query_feature_width : query_feature_width + key_feature_width
    ].reshape(decode_row_count, token_steps, KEY_VALUE_HEADS, ATTN_DEPTH)
    value_rows = received_shards[..., query_feature_width + key_feature_width :].reshape(
        decode_row_count, token_steps, KEY_VALUE_HEADS, ATTN_DEPTH
    )
    positions = (
        stored_extent_per_sequence[:, None] + jnp.arange(token_steps, dtype=jnp.int32)[None, :]
    ).astype(jnp.float32)[:, :, None]
    rot_query = rotate(
        rms_norm(query.astype(jnp.float32), probe_norm_multiplier), positions
    ).astype(jnp.bfloat16)
    rot_keys = rotate(
        rms_norm(key_rows.astype(jnp.float32), lookup_norm_multiplier), positions
    ).astype(jnp.bfloat16)
    attended = attend(
        rot_query,
        rot_keys,
        value_rows,
        stored_rotated_lookups,
        stored_contents,
        stored_extent_per_sequence,
    )
    returned = lax.all_to_all(attended, "tensor", split_axis=2, concat_axis=0, tiled=True)
    amount = decode_row_count * lax.axis_size("tensor")
    flattened_rows = returned.reshape(amount * token_steps, returned.shape[2])
    total = lax.psum_scatter(
        jnp.dot(flattened_rows, merged_projection_back, preferred_element_type=jnp.float32).reshape(
            amount, token_steps, width
        ),
        "tensor",
        scatter_dimension=0,
        tiled=True,
    )
    return total.astype(jnp.bfloat16)


BF16 = jnp.bfloat16
F32 = jnp.float32
MESH = pl.DeviceIdType.MESH


def dot_nn(a, b):
    return jnp.dot(a, b, preferred_element_type=F32)


def dot_nt(a, b):
    return lax.dot_general(a, b, (((1,), (1,)), ((), ())), preferred_element_type=F32)


def fused_kernel(
    n,
    x_ref, gain_ref, wq_ref, wk_ref, wv_ref, wo_ref, qgain_ref, kgain_ref,
    a_ref, b_ref, c_ref, d_ref, kc_ref, vc_ref, len_ref,
    out_ref,
    xs, w, wo, kbuf, vbuf, a2, b1, c2, d2, ts, us, acc, qs, qr, att_src, ar, abf, py, ry, own, ps, rr, half_out, half_in,
    loc, x_s, x_f, x_r, t_s, t_r, q_s, q_r, a_s, a_f, a_r, u_s, u_r, y_s, y_r, p_s, p_r, m_s, m_r,
):
    i = lax.axis_index("tensor")
    r = lax.axis_index("replica")
    o = 1 - r
    me = 2 * i + r
    width = x_ref.shape[2]
    qcols = w.shape[1] - ATTN_DEPTH
    ocols = wo.shape[1]
    chunk = rr.shape[3]
    chunks = ocols // chunk
    slots_len = kc_ref.shape[2]

    def peer(j, core):
        return {"tensor": j, "replica": core}

    def remote(src, dst, ssem, rsem, j, core):
        return pltpu.make_async_remote_copy(
            src_ref=src, dst_ref=dst, send_sem=ssem, recv_sem=rsem,
            device_id=peer(j, core), device_id_type=MESH,
        )

    def ahead(d):
        return lax.rem(i + d, n)

    def behind(d):
        return lax.rem(i + n - d, n)

    nz = n // 2
    z, y = i // 2, lax.rem(i, 2)
    side = i + 1 - 2 * y

    def z_ahead(d):
        return 2 * lax.rem(z + d, nz) + y

    def z_behind(d):
        return 2 * lax.rem(z + nz - d, nz) + y

    barrier = pltpu.get_barrier_semaphore()

    @pl.loop(1, 2 * n)
    def _(d):
        dev = lax.rem(me + d, 2 * n)
        pl.semaphore_signal(barrier, inc=1, device_id=peer(dev // 2, lax.rem(dev, 2)), device_id_type=MESH)

    cp_w = pltpu.make_async_copy(wq_ref.at[:, pl.ds(pl.multiple_of(r * qcols, 128), qcols)], w.at[:, pl.ds(0, qcols)], loc.at[0])
    cp_w.start()
    wkv_dst = w.at[:, pl.ds(qcols, ATTN_DEPTH)]
    cp_k = pltpu.make_async_copy(wk_ref, wkv_dst, loc.at[1])
    cp_v = pltpu.make_async_copy(wv_ref, wkv_dst, loc.at[1])

    @pl.when(r == 0)
    def _():
        cp_k.start()

    @pl.when(r == 1)
    def _():
        cp_v.start()

    small = [
        pltpu.make_async_copy(a_ref, a2.at[r], loc.at[2]),
        pltpu.make_async_copy(b_ref, b1, loc.at[3]),
        pltpu.make_async_copy(c_ref, c2.at[r], loc.at[4]),
        pltpu.make_async_copy(d_ref, d2.at[r], loc.at[5]),
    ]
    caches = []
    for b in range(2):
        caches.append(pltpu.make_async_copy(kc_ref.at[b], kbuf.at[:, pl.ds(b * slots_len, slots_len), :], loc.at[6 + b]))
        caches.append(pltpu.make_async_copy(vc_ref.at[b], vbuf.at[:, pl.ds(b * slots_len, slots_len), :], loc.at[8 + b]))
    cp_wo = pltpu.make_async_copy(wo_ref.at[:, pl.ds(pl.multiple_of(r * ocols, 128), ocols)], wo, loc.at[10])
    for cp in small + caches + [cp_wo]:
        cp.start()

    xf = jnp.concatenate([x_ref[0].astype(F32), x_ref[1].astype(F32)], axis=0)
    inv = lax.rsqrt(jnp.mean(xf * xf, axis=-1, keepdims=True) + 1e-06)
    xs[me] = (xf * inv * gain_ref[...]).astype(BF16)

    pl.semaphore_wait(barrier, 2 * n - 1)

    def x_direct(d):
        return remote(xs.at[me], xs.at[me], x_s.at[d], x_r.at[me], z_ahead(d), r)

    x_side = remote(xs.at[me], xs.at[me], x_s.at[0], x_r.at[me], side, r)
    x_pair = remote(xs.at[me], xs.at[me], x_s.at[nz], x_r.at[me], i, o)

    @pl.loop(1, nz)
    def _(d):
        x_direct(d).start()

    x_side.start()
    x_pair.start()
    lora_pair = [
        remote(a_ref, a2.at[r], m_s.at[0], m_r.at[0], i, o),
        remote(c_ref, c2.at[r], m_s.at[1], m_r.at[1], i, o),
        remote(d_ref, d2.at[r], m_s.at[2], m_r.at[2], i, o),
    ]
    for cp in lora_pair:
        cp.start()

    row8 = lax.broadcasted_iota(jnp.int32, (8, ATTN_DEPTH), 0)
    lane8 = lax.broadcasted_iota(jnp.int32, (8, ATTN_DEPTH), 1)
    len0, len1 = len_ref[0], len_ref[1]
    pos = (jnp.where(row8 < 4, len0, len1) + lax.rem(row8, 4)).astype(F32)
    half_i = lax.rem(lane8, ATTN_DEPTH // 2).astype(F32)
    freq = jnp.exp(half_i * (-2.0 / ATTN_DEPTH * math.log(rope_base)))
    ang = pos * freq
    cos8 = jnp.cos(ang)
    sin8 = jnp.where(lane8 < ATTN_DEPTH // 2, -jnp.sin(ang), jnp.sin(ang))
    kbuf[:, pl.ds(2 * slots_len, 128), :] = jnp.zeros((n, 128, ATTN_DEPTH), BF16)
    vbuf[:, pl.ds(2 * slots_len, 128), :] = jnp.zeros((n, 128, ATTN_DEPTH), BF16)

    def x_fwd(k, s, j, core):
        return remote(xs.at[s], xs.at[s], x_f.at[k], x_r.at[s], j, core)

    def x_fwds(d):
        s = 2 * z_behind(d) + r
        return x_fwd(2 * d - 2, s, side, r), x_fwd(2 * d - 1, s, i, o)

    def x_side_fwd(d):
        s = 2 * (z_behind(d) + side - i) + r
        return x_fwd(2 * nz - 2 + d, s, i, o)

    def x_arr(s):
        return remote(xs.at[s], xs.at[s], x_s.at[0], x_r.at[s], i, o)

    @pl.loop(1, nz)
    def _(d):
        x_arr(2 * z_behind(d) + r).wait_recv()
        for cp in x_fwds(d):
            cp.start()

    @pl.loop(0, nz)
    def _(d):
        x_arr(2 * (z_behind(d) + side - i) + r).wait_recv()
        x_side_fwd(d).start()

    @pl.loop(0, n)
    def _(d):
        x_arr(2 * behind(d) + o).wait_recv()

    def x_rows(k):
        v = xs[:, :, pl.ds(pl.multiple_of(k * 640, 128), 640)]
        return v.astype(F32).reshape(16 * 8, 640).astype(BF16)

    def pack(t):
        h = t.shape[0] // 2
        return jnp.concatenate([t[:h], t[h:]], axis=1)

    def unpack(t):
        h = t.shape[1] // 2
        return jnp.concatenate([t[:, :h], t[:, h:]], axis=0)

    small[0].wait()
    lora_pair[0].wait_recv()
    t_mine = dot_nt(x_rows(i), jnp.concatenate([a2[0], a2[1]], axis=1))
    ts[i] = pack(t_mine).astype(BF16)

    def t_copy(d):
        return remote(ts.at[i], ts.at[i], t_s.at[d], t_r.at[i], ahead(d), r)

    def t_arr(s):
        return remote(ts.at[s], ts.at[s], t_s.at[0], t_r.at[s], i, o)

    @pl.loop(1, n)
    def _(d):
        t_copy(d).start()

    cp_w.wait()
    cp_k.wait()
    acc[...] = jnp.zeros_like(acc)

    @pl.loop(0, width // 640)
    def _(k):
        acc[...] += dot_nn(x_rows(k), w[pl.ds(pl.multiple_of(k * 640, 128), 640), :])

    @pl.loop(1, n)
    def _(d):
        t_arr(behind(d)).wait_recv()

    small[1].wait()
    t_all = unpack(jnp.sum(ts[...].astype(F32), axis=0)).astype(BF16)
    acc[:, pl.ds(0, qcols)] += delta_multiplier * dot_nn(t_all, b1[...])
    proj = acc[...].reshape(16, 8, w.shape[1]).astype(BF16)
    qs[...] = proj

    def q_copy(d):
        dev = lax.rem(me + d, 2 * n)
        return remote(qs.at[dev], qr.at[me], q_s.at[d], q_r.at[me], dev // 2, lax.rem(dev, 2))

    def q_arr(s):
        return remote(qr.at[s], qr.at[s], q_s.at[0], q_r.at[s], i, o)

    @pl.loop(1, 2 * n)
    def _(d):
        q_copy(d).start()

    qr[me] = qs[me]

    @pl.loop(1, 2 * n)
    def _(d):
        q_arr(lax.rem(me + 2 * n - d, 2 * n)).wait_recv()

    for cp in caches:
        cp.wait()

    heads = qcols // ATTN_DEPTH
    rows = 2 * heads * 8
    cos_q = jnp.concatenate([cos8] * (2 * heads), axis=0)
    sin_q = jnp.concatenate([sin8] * (2 * heads), axis=0)
    rb = lax.rem(lax.broadcasted_iota(jnp.int32, (rows, slots_len), 0), 8) // 4
    cache_ok = lax.broadcasted_iota(jnp.int32, (rows, slots_len), 1) < jnp.where(rb == 0, len0, len1)
    first_row = rb == 0
    fr = lax.rem(lax.broadcasted_iota(jnp.int32, (rows, 128), 0), 8)
    fc = lax.broadcasted_iota(jnp.int32, (rows, 128), 1)
    fresh_ok = (fc // 4 == fr // 4) & (lax.rem(fc, 4) <= lax.rem(fr, 4))
    scale = 1.0 / ATTN_DEPTH**0.5

    def norm_rotate(v, gain, cosine, sine):
        v = v * lax.rsqrt(jnp.mean(v * v, axis=-1, keepdims=True) + 1e-06) * gain
        return (v * cosine + pltpu.roll(v, ATTN_DEPTH // 2, 1) * sine).astype(BF16)

    def a_direct(j, d):
        return remote(att_src.at[j], ar.at[me], a_s.at[d], a_r.at[me], j, r)

    a_pair = remote(ar.at[me], ar.at[me], a_s.at[0], a_r.at[me], i, o)

    def head_group(j):
        q0 = qr[2 * j].astype(F32)
        q1 = qr[2 * j + 1].astype(F32)
        qh = jnp.concatenate(
            [q[:, h * ATTN_DEPTH : (h + 1) * ATTN_DEPTH] for q in (q0, q1) for h in range(heads)], axis=0
        )
        q = norm_rotate(qh, qgain_ref[...], cos_q, sin_q)
        kn = norm_rotate(q0[:, qcols:], kgain_ref[...], cos8, sin8).astype(F32)
        pad = jnp.zeros((8, ATTN_DEPTH), F32)
        kbuf[j, pl.ds(2 * slots_len, 16), :] = jnp.concatenate([kn, pad], axis=0).astype(BF16)
        vbuf[j, pl.ds(2 * slots_len, 16), :] = jnp.concatenate([q1[:, qcols:], pad], axis=0).astype(BF16)
        s = dot_nt(q, kbuf[j]) * scale
        cached = jnp.where(first_row, s[:, :slots_len], s[:, slots_len : 2 * slots_len])
        ec = jnp.where(cache_ok, jnp.exp(cached), 0.0)
        ef = jnp.where(fresh_ok, jnp.exp(s[:, 2 * slots_len :]), 0.0)
        denom = jnp.sum(ec, axis=-1, keepdims=True) + jnp.sum(ef, axis=-1, keepdims=True)
        wc = ec / denom
        wf = ef / denom
        wgt = jnp.concatenate(
            [jnp.where(first_row, wc, 0.0), jnp.where(first_row, 0.0, wc), wf], axis=1
        ).astype(BF16)
        o_ = dot_nn(wgt, vbuf[j])
        return jnp.concatenate([o_[h * 8 : (h + 1) * 8] for h in range(2 * heads)], axis=1).astype(BF16)

    @pl.loop(1, n)
    def _(d):
        j = ahead(d)
        att_src[j] = head_group(j)
        a_direct(j, d).start()

    ar[me] = head_group(i)
    a_pair.start()

    def a_arr(s):
        return remote(ar.at[s], ar.at[s], a_s.at[0], a_r.at[s], i, o)

    def a_fwd(d, j):
        s = 2 * j + r
        return remote(ar.at[s], ar.at[s], a_f.at[d], a_r.at[s], i, o)

    @pl.loop(1, n)
    def _(d):
        j = behind(d)
        a_arr(2 * j + r).wait_recv()
        a_fwd(d, j).start()

    @pl.loop(0, n)
    def _(d):
        a_arr(2 * behind(d) + o).wait_recv()

    abf[...] = ar[...].astype(F32).reshape(16 * 8, ar.shape[2]).astype(BF16)
    small[2].wait()
    lora_pair[1].wait_recv()
    us[i] = pack(dot_nt(abf[...], jnp.concatenate([c2[0], c2[1]], axis=1))).astype(BF16)

    def u_copy(d):
        return remote(us.at[i], us.at[i], u_s.at[d], u_r.at[i], ahead(d), r)

    def u_arr(s):
        return remote(us.at[s], us.at[s], u_s.at[0], u_r.at[s], i, o)

    @pl.loop(1, n)
    def _(d):
        u_copy(d).start()

    cp_wo.wait()
    small[3].wait()
    lora_pair[2].wait_recv()
    own_chunk = lax.rem(i, chunks)

    def order(k):
        return lax.rem(2 * (i // 2) + 2 + k, chunks)

    def y_copy(cc):
        return remote(py.at[cc], ry.at[cc], y_s.at[cc], y_r.at[cc], side, r)

    def p_copy(cc, d):
        j = z_ahead(d)
        return remote(ps.at[cc, j // 2], rr.at[cc, z], p_s.at[cc, d], p_r.at[cc, z], j, r)

    def p_arr(cc, s):
        return remote(rr.at[cc, s], rr.at[cc, s], p_s.at[0, 0], p_r.at[cc, s], i, o)

    def base(cc):
        return dot_nn(abf[...], wo[:, pl.ds(pl.multiple_of(cc * chunk, 128), chunk)])

    def ship(cc, part):
        v = part.reshape(nz, 2, 16, chunk)
        own[cc] = jnp.where(y == 0, v[:, 0], v[:, 1])
        py[cc] = jnp.where(y == 0, v[:, 1], v[:, 0]).astype(BF16)
        y_copy(cc).start()

    def merge(cc):
        y_copy(cc).wait_recv()
        v = own[cc] + ry[cc].astype(F32)
        own[cc] = v
        ps[cc] = v.astype(BF16)

        @pl.loop(1, nz)
        def _(d):
            p_copy(cc, d).start()

    ship(order(0), base(order(0)))
    ship(order(1), base(order(1)))
    merge(order(0))

    @pl.loop(1, n)
    def _(d):
        u_arr(behind(d)).wait_recv()

    u_all = unpack(jnp.sum(us[...].astype(F32), axis=0)).astype(BF16)
    low = dot_nn(u_all, jnp.concatenate([d2[0], d2[1]], axis=1))
    for k in (2, 3):
        cc = order(k)
        mult = jnp.where((cc == own_chunk) & (i // chunks == r), delta_multiplier, 0.0)
        ship(cc, base(cc) + mult * low)
        merge(order(k - 1))
    merge(order(3))

    @pl.loop(0, chunks)
    def _(k):
        cc = order(k)
        total = own[cc, z]
        for d in range(1, nz):
            s = z_behind(d) // 2
            p_arr(cc, s).wait_recv()
            total = total + rr[cc, s].astype(F32)
        total = total.reshape(2, 8, chunk)
        mine = jnp.where(r == 0, total[0], total[1])
        theirs = jnp.where(r == 0, total[1], total[0])
        half_out[cc] = theirs
        out_ref[:, pl.ds(pl.multiple_of(r * ocols + cc * chunk, 128), chunk)] = mine.astype(BF16)
        remote(half_out.at[cc], half_in.at[cc], m_s.at[3 + cc], m_r.at[3 + cc], i, o).start()

    @pl.loop(0, chunks)
    def _(k):
        cc = order(k)
        remote(half_out.at[cc], half_in.at[cc], m_s.at[3 + cc], m_r.at[3 + cc], i, o).wait()
        out_ref[:, pl.ds(pl.multiple_of(o * ocols + cc * chunk, 128), chunk)] = half_in[cc].astype(BF16)

    for cp in lora_pair:
        cp.wait_send()
    x_pair.wait_send()
    x_side.wait_send()
    a_pair.wait_send()

    @pl.loop(1, nz)
    def _(d):
        x_direct(d).wait_send()
        for cp in x_fwds(d):
            cp.wait_send()
        for cc in range(chunks):
            p_copy(cc, d).wait_send()

    @pl.loop(0, nz)
    def _(d):
        x_side_fwd(d).wait_send()
        y_copy(d).wait_send()

    @pl.loop(1, n)
    def _(d):
        t_copy(d).wait_send()
        a_direct(ahead(d), d).wait_send()
        a_fwd(d, behind(d)).wait_send()
        u_copy(d).wait_send()

    @pl.loop(1, 2 * n)
    def _(d):
        q_copy(d).wait_send()


def fused_body(
    n,
    fresh_activations,
    entry_norm_multiplier,
    base_probe_projection,
    lookup_projection,
    contents_projection,
    base_result_projection,
    probe_norm_multiplier,
    lookup_norm_multiplier,
    probe_narrowing_matrix,
    probe_widening_matrix,
    result_narrowing_matrix,
    result_widening_matrix,
    stored_rotated_lookups,
    stored_contents,
    stored_extent_per_sequence,
):
    rows_dev, steps, width = fresh_activations.shape
    rows = rows_dev * steps
    qcols = base_probe_projection.shape[1] // 2
    ocols = width // 2
    feats = base_result_projection.shape[0]
    rank = probe_narrowing_matrix.shape[1]
    part, up = probe_narrowing_matrix.shape[0], probe_widening_matrix.shape[0]
    slots = stored_rotated_lookups.shape[2]
    chunk = 2 * part
    chunks = ocols // chunk
    vmem = pl.BlockSpec(memory_space=pltpu.VMEM)
    hbm = pl.BlockSpec(memory_space=pl.ANY)
    smem = pl.BlockSpec(memory_space=pltpu.SMEM)
    dma = pltpu.SemaphoreType.DMA
    out = pl.pallas_call(
        functools.partial(fused_kernel, n),
        out_shape=jax.ShapeDtypeStruct((rows, width), BF16),
        in_specs=[vmem, vmem, hbm, hbm, hbm, hbm, vmem, vmem, hbm, hbm, hbm, hbm, hbm, hbm, smem],
        out_specs=vmem,
        scratch_shapes=[
            pltpu.VMEM((2 * n, rows, width), BF16),
            pltpu.VMEM((width, qcols + ATTN_DEPTH), BF16),
            pltpu.VMEM((feats, ocols), BF16),
            pltpu.VMEM((n, 2 * slots + 128, ATTN_DEPTH), BF16),
            pltpu.VMEM((n, 2 * slots + 128, ATTN_DEPTH), BF16),
            pltpu.VMEM((2, rank, part), BF16),
            pltpu.VMEM((rank, up), BF16),
            pltpu.VMEM((2, rank, up), BF16),
            pltpu.VMEM((2, rank, part), BF16),
            pltpu.VMEM((n, n * rows, 2 * rank), BF16),
            pltpu.VMEM((n, n * rows, 2 * rank), BF16),
            pltpu.VMEM((2 * n * rows, qcols + ATTN_DEPTH), F32),
            pltpu.VMEM((2 * n, rows, qcols + ATTN_DEPTH), BF16),
            pltpu.VMEM((2 * n, rows, qcols + ATTN_DEPTH), BF16),
            pltpu.VMEM((n, rows, feats), BF16),
            pltpu.VMEM((2 * n, rows, feats), BF16),
            pltpu.VMEM((2 * n * rows, feats), BF16),
            *[pltpu.VMEM((chunks, n // 2, 2 * rows, chunk), dt) for dt in (BF16, BF16, F32, BF16, BF16)],
            pltpu.VMEM((chunks, rows, chunk), F32),
            pltpu.VMEM((chunks, rows, chunk), F32),
            dma((11,)),
            dma((n,)), dma((2 * n,)), dma((2 * n,)),
            dma((n,)), dma((n,)),
            dma((2 * n,)), dma((2 * n,)),
            dma((n,)), dma((n,)), dma((2 * n,)),
            dma((n,)), dma((n,)),
            dma((chunks,)), dma((chunks,)),
            dma((chunks, n // 2)), dma((chunks, n // 2)),
            dma((3 + chunks,)), dma((3 + chunks,)),
        ],
        compiler_params=pltpu.CompilerParams(
            collective_id=0, has_side_effects=True, vmem_limit_bytes=56 * 1024 * 1024
        ),
        name="fused_attention_sync",
    )(
        fresh_activations,
        entry_norm_multiplier.reshape(1, width),
        base_probe_projection,
        lookup_projection,
        contents_projection,
        base_result_projection,
        probe_norm_multiplier.reshape(1, ATTN_DEPTH),
        lookup_norm_multiplier.reshape(1, ATTN_DEPTH),
        probe_narrowing_matrix.T,
        probe_widening_matrix.T,
        result_narrowing_matrix.T,
        result_widening_matrix.T,
        stored_rotated_lookups,
        stored_contents,
        stored_extent_per_sequence,
    )
    return out.reshape(rows_dev, steps, width)


def solution(mesh):
    n = mesh.shape["tensor"]
    fits = n == KEY_VALUE_HEADS and mesh.shape["replica"] == 2
    return jax.shard_map(
        functools.partial(fused_body, n) if fits else body,
        mesh=mesh,
        in_specs=(
            P(("groups", "tensor", "replica"), None, None),
            P("groups"),
            P("groups", "tensor"),
            P("groups", "tensor"),
            P("groups", "tensor"),
            P(("groups", "tensor"), None),
            P("groups"),
            P("groups"),
            P(("groups", "tensor", "replica"), None),
            P(("groups", "tensor", "replica"), None),
            P(("groups", "tensor", "replica"), None),
            P(("groups", "tensor", "replica"), None),
            P(("groups", "tensor", "replica"), None, None, None),
            P(("groups", "tensor", "replica"), None, None, None),
            P(("groups", "tensor", "replica")),
        ),
        out_specs=P(("groups", "tensor", "replica"), None, None),
        check_vma=False,
    )
```
